32 devices in a mesh: grp: 2 (over x), req: 16 (over z, y, core).
Axes of the slice: x: 2, y: 2, z: 4, core: 2. Of those that a mesh axis runs over, the one named last changes fastest.
Arguments:
- tokens: bfloat16 [16384, 8192], P(('grp', 'req')), parts along dimension 0, may hold values from -6 to 6
- key_value_weight: bfloat16 [8192, 1024], P('req'), may hold values from -0.0625 to 0.0625
- adapter_down_weight: bfloat16 [64, 8192, 16], P(None, 'req'), may hold values from -0.0625 to 0.0625
- adapter_up_weight: bfloat16 [64, 1024, 16], P(None, 'req'), may hold values from -1.5 to 1.5
- request_adapter: int32 [64], P('grp'), parts along dimension 0, may hold values from 0 to 63
- adapter_table_row: int32 [64], replicated, may hold values from 0 to 63, each once
- lengths: int32 [64], P(('grp', 'req')), parts along dimension 0, may hold values from 1 to 256, as said below
Outputs:
- kv_out: bfloat16 [16384, 1024], P(('grp', 'req')), parts along dimension 0
The draws below stay inside these ranges and needn't reach their ends.
There are 2 independent parts, one for each index of `grp`. The reference program is written for one: setup_inputs(seed, part) draws one part's arguments, and reference() takes and returns one part's arrays. A program takes and returns all parts, laid end to end along the dimension named above; an argument that names none is the same for every part. Nothing has to cross between parts.
Inputs may be any that keep to these rules, and one draw needn't show every extreme that they name: `lengths`: some request has exactly 256 live rows.
All inputs are finite; a program needn't handle non-finite values.
Results may differ from the reference program's by a relative error of at most 0.003.
Values may be sent and summed in bfloat16 or wider, within the bound.
A program may use at most 128 MiB of HBM per device.

```python
import math
import jax
import jax.numpy as jnp
import numpy as np
from jax import lax

MODEL_WIDTH = 8192
ADAPTER_RANK = 16
REQ_LEN = 256
KEY_VALUE_WIDTH = 1024
ADAPTER_COUNT = 64
REQUESTS = 32
TOKENS = 8192


def draw_lengths(key, part):
    key = jax.random.fold_in(key, 7)
    first_key, second_key = jax.random.split(key)
    drawn = jax.random.randint(first_key, (REQUESTS,), 1, REQ_LEN + 1, dtype=jnp.int32)
    chosen = jax.random.randint(second_key, (), 0, REQUESTS, dtype=jnp.int32)
    return drawn.at[chosen].set(REQ_LEN)


def plant(values, stream_key, smallest, top_value):
    longest = values.shape.index(max(values.shape))
    spots = []
    for shift in (0, 1):
        where = [jax.random.randint(jax.random.fold_in(stream_key, axis), (), 0, length) for axis, length in enumerate(values.shape)]
        where[longest] = (where[longest] + shift) % values.shape[longest]
        spots.append(tuple(where))
    return values.at[spots[0]].set(smallest).at[spots[1]].set(top_value)


def block_scale(own_key, extent, pieces, least, high):
    gain = 1.0
    for dim, parts in pieces:
        draws = jax.random.uniform(jax.random.fold_in(jax.random.fold_in(own_key, 6), dim), (parts,), jnp.float32, least / len(pieces), high / len(pieces))
        gain = gain * jnp.repeat(jnp.exp(draws), extent[dim] // parts).reshape((-1,) + (1,) * (len(extent) - 1 - dim))
    return gain


def cumulative_ranks(amount, slope):
    loads = [(1 << 20) // math.isqrt(grade ** slope) + 1 for grade in range(1, amount + 1)]
    deviation = 1 + sum(loads) // (1 << 30)
    return np.cumsum(np.array([max(1, weight // deviation) for weight in loads]))


def ranked_ids(own_key, dims, amount, skew):
    table = cumulative_ranks(amount, skew)
    pick = jax.random.randint(jax.random.fold_in(own_key, 1), dims, 0, int(table[amount - 1]))
    rank = jnp.searchsorted(jnp.asarray(table, jnp.int32), pick, side="right")
    return jax.random.permutation(jax.random.fold_in(own_key, 2), amount)[rank].astype(jnp.int32)


def centred(own_key, shape, spread, most, shards=(), held_as=jnp.bfloat16):
    entries = jax.random.normal(own_key, shape, jnp.float32) * spread
    if len(shards) > 0:
        entries = block_scale(own_key, shape, shards, -0.22, 0.18) * entries
    return jnp.clip(entries, min=-most, max=most).astype(held_as)


def setup_inputs(seed: int = 0, part: int = 0) -> dict:
    arg_keys = jax.random.split(jax.random.key(seed), 8)
    part_splits = jax.random.split(jax.random.fold_in(arg_keys[7], part), 8)
    tokens = centred(part_splits[0], (TOKENS, MODEL_WIDTH), 1.0, 6.0, ((0, 16),))
    key_value_weight = centred(arg_keys[1], (MODEL_WIDTH, KEY_VALUE_WIDTH), MODEL_WIDTH ** -0.5, 0.0625, ((0, 16),))
    adapter_down_weight = centred(arg_keys[2], (ADAPTER_COUNT, MODEL_WIDTH, ADAPTER_RANK), MODEL_WIDTH ** -0.5, 0.0625, ((1, 16),))
    adapter_up_weight = centred(arg_keys[3], (ADAPTER_COUNT, KEY_VALUE_WIDTH, ADAPTER_RANK), ADAPTER_RANK ** -0.5, 1.5, ((1, 16),))
    request_adapter = plant(ranked_ids(part_splits[4], (REQUESTS,), ADAPTER_COUNT, 2), jax.random.fold_in(part_splits[4], 3), 0, ADAPTER_COUNT - 1).astype(jnp.int32)
    adapter_table_row = jax.random.permutation(arg_keys[5], ADAPTER_COUNT).astype(jnp.int32)
    lengths = draw_lengths(jax.random.fold_in(jax.random.fold_in(arg_keys[7], part), 71), part)
    return dict(tokens=tokens, key_value_weight=key_value_weight, adapter_down_weight=adapter_down_weight, adapter_up_weight=adapter_up_weight, request_adapter=request_adapter, adapter_table_row=adapter_table_row, lengths=lengths)


def reference(tokens, key_value_weight, adapter_down_weight, adapter_up_weight, request_adapter, adapter_table_row, lengths):
    row_of = adapter_table_row[request_adapter].astype(jnp.int32)
    base = jnp.dot(tokens, key_value_weight, preferred_element_type=jnp.float32)
    grouped = tokens.reshape(REQUESTS, REQ_LEN, MODEL_WIDTH)

    def one_request(pair):
        rows, slot_row = pair
        down_matrix = adapter_down_weight[slot_row]
        up_matrix = adapter_up_weight[slot_row]
        reduced = jnp.dot(rows, down_matrix, preferred_element_type=jnp.float32).astype(jnp.bfloat16)
        return jnp.dot(reduced, up_matrix.T, preferred_element_type=jnp.float32)

    adapter_term = lax.map(one_request, (grouped, row_of)).reshape(TOKENS, KEY_VALUE_WIDTH)
    position = jnp.arange(REQ_LEN, dtype=jnp.int32)
    live_rows = (position[None, :] < lengths[:, None]).reshape(TOKENS, 1)
    mixed = jnp.where(live_rows, base + 0.5 * adapter_term, jnp.zeros_like(base))
    return mixed.astype(jnp.bfloat16)
```

```python
import jax
import jax.numpy as jnp
from jax import lax
from jax.experimental import pallas as pl
from jax.experimental.pallas import tpu as pltpu
from jax.sharding import PartitionSpec as P

MESH = pl.DeviceIdType.MESH


def gather_kernel(
    req_ref, table_ref, tok_hbm, w_hbm, down_hbm, up_hbm, out_ref,
    wfull, tok, acc, down_tab, up_tab, down_stage, up_stage, down_in, up_in, up_all, red,
    local_sem, recv_sem, send_sem, ad_send, ad_recv,
):
    depth, width = w_hbm.shape
    rows = tok.shape[0]
    per = req_ref.shape[0] // 16
    rank = down_tab.shape[1]
    side = depth * 3 // 8
    mid = depth - 2 * side
    x = lax.axis_index("grp")
    me = lax.axis_index("req")
    c = lax.rem(me, 2)
    y = lax.rem(lax.div(me, 2), 2)
    z = lax.div(me, 4)
    flip = lax.div(z, 2)
    zz = z + flip * (3 - 2 * z)
    inner = z + 1 - 2 * flip
    outer = z - 1 + 2 * flip
    inside = zz == 1
    order = []
    for o in (zz, 1 - zz, 2, 3):
        order.append(o + flip * (3 - 2 * o))

    def chip(far, k):
        yy = (1 - y) if far else y
        return order[k] * 2 + yy

    def device(xx, yy, zz_, cc):
        return (xx, (zz_ * 2 + yy) * 2 + cc)

    z_in = device(x, y, inner, c)
    z_out = device(x, y, outer, c)
    y_dev = device(x, 1 - y, z, c)
    x_dev = device(1 - x, y, z, c)
    sib = device(x, y, z, 1 - c)

    tok_copy = pltpu.make_async_copy(tok_hbm, tok, local_sem.at[0])
    own_rows = wfull.at[chip(0, 0), pl.ds(pl.multiple_of(c * depth, depth), depth)]
    own_copy = pltpu.make_async_copy(w_hbm, own_rows, local_sem.at[1])
    down_copy = pltpu.make_async_copy(down_hbm, down_tab, local_sem.at[2])
    up_copy = pltpu.make_async_copy(up_hbm, up_tab, local_sem.at[3])
    down_copy.start()
    up_copy.start()
    own_copy.start()
    tok_copy.start()

    barrier = pltpu.get_barrier_semaphore()

    def greet(i, carry):
        pl.semaphore_signal(
            barrier, inc=1, device_id=(x, lax.rem(me + i, 16)), device_id_type=MESH
        )
        return carry

    lax.fori_loop(1, 16, greet, 0)
    pl.semaphore_signal(barrier, inc=1, device_id=x_dev, device_id_type=MESH)
    pl.semaphore_wait(barrier, 16)

    starts = (x * (side + mid), side, (1 - x) * (side + mid))
    counts = (side, mid, side)
    pending = []

    def piece(part, m, cc):
        at = pl.multiple_of(cc * depth + starts[part], 64)
        return wfull.at[m, pl.ds(at, counts[part])]

    def send(part, m, dev, landing=None, own=False, when=None):
        here = piece(part, m, c)
        if own:
            src = w_hbm.at[pl.ds(pl.multiple_of(starts[part], 64), counts[part])]
        else:
            src = here
        copy = pltpu.make_async_remote_copy(
            src_ref=src,
            dst_ref=here,
            send_sem=send_sem.at[len(pending)],
            recv_sem=recv_sem.at[part if landing is None else landing, m, c],
            device_id=dev,
            device_id_type=MESH,
        )
        pending.append((copy, when))
        if when is None:
            copy.start()
        else:
            pl.when(when)(copy.start)

    def arrived(part, m, cc):
        here = piece(part, m, cc)
        pltpu.make_async_remote_copy(
            src_ref=here,
            dst_ref=here,
            send_sem=send_sem.at[0],
            recv_sem=recv_sem.at[part, m, cc],
            device_id=sib,
            device_id_type=MESH,
        ).wait_recv()

    def multiply(m):
        cols = pl.ds(pl.multiple_of(m * 2 * depth, 2 * depth), 2 * depth)

        def tile(j, carry):
            at = pl.ds(pl.multiple_of(j * 256, 256), 256)
            acc[:, at] += jnp.dot(
                tok[:, cols], wfull[m, :, at], preferred_element_type=jnp.float32
            )
            return carry

        lax.fori_loop(0, width // 256, tile, 0)

    def sibling_done(m):
        for part in range(3):
            arrived(part, m, 1 - c)

    mine = chip(0, 0)
    for part in (0, 1):
        send(part, mine, z_in, own=True)
        send(part, mine, z_out, own=True, when=inside)
        send(part, mine, y_dev, own=True)
    for part in range(3):
        send(part, mine, sib, own=True)

    down_copy.wait()
    up_copy.wait()

    def pick(q, carry):
        row = table_ref[req_ref[q]]
        down_stage[q] = down_tab[row]
        up_stage[q] = up_tab[row]
        return carry

    lax.fori_loop(0, per * 16, pick, 0)

    def adapter_copies(i, dest, source):
        to = pl.ds(dest * per, per)
        return (
            pltpu.make_async_remote_copy(
                src_ref=down_stage.at[to],
                dst_ref=down_in.at[source],
                send_sem=ad_send.at[0, i],
                recv_sem=ad_recv.at[0, source],
                device_id=(x, dest),
                device_id_type=MESH,
            ),
            pltpu.make_async_remote_copy(
                src_ref=up_stage.at[to],
                dst_ref=up_in.at[source],
                send_sem=ad_send.at[1, i],
                recv_sem=ad_recv.at[1, source],
                device_id=(x, dest),
                device_id_type=MESH,
            ),
        )

    def ship(i, carry):
        for copy in adapter_copies(i, lax.rem(me + i, 16), me):
            copy.start()
        return carry

    lax.fori_loop(1, 16, ship, 0)
    down_in[me] = down_stage[pl.ds(me * per, per)]
    up_in[me] = up_stage[pl.ds(me * per, per)]
    acc[...] = jnp.zeros_like(acc)
    red[...] = jnp.zeros_like(red)
    own_copy.wait()
    tok_copy.wait()

    def adapters():
        def landed(i, carry):
            for copy in adapter_copies(i, me, lax.rem(me + 16 - i, 16)):
                copy.wait_recv()
            return carry

        lax.fori_loop(1, 16, landed, 0)

        def reduce(s, carry):
            cols = pl.ds(pl.multiple_of(s * depth, depth), depth)
            red[...] += lax.dot_general(
                tok[:, cols],
                down_in[s].reshape(per * rank, depth),
                (((1,), (1,)), ((), ())),
                preferred_element_type=jnp.float32,
            )
            return carry

        lax.fori_loop(0, 16, reduce, 0)
        span = rows // per
        row_request = lax.broadcasted_iota(jnp.int32, red.shape, 0) // span
        map_request = lax.broadcasted_iota(jnp.int32, red.shape, 1) // rank
        kept = jnp.where(row_request == map_request, red[...], 0.0).astype(jnp.bfloat16)
        part = up_in.shape[3]
        for s in range(0, 16, 2):
            pair = [up_in[s + j].reshape(per * rank, part) for j in range(2)]
            up_all[:, s * part:(s + 2) * part] = jnp.concatenate(pair, axis=1)

        def tile(j, carry):
            at = pl.ds(pl.multiple_of(j * 256, 256), 256)
            acc[:, at] += 0.5 * jnp.dot(
                kept, up_all[:, at], preferred_element_type=jnp.float32
            )
            return carry

        lax.fori_loop(0, width // 256, tile, 0)

    def from_x(far, k):
        m = chip(far, k)
        arrived(2, m, c)
        send(2, m, sib)

    for k in range(1, 4):
        near, other = chip(0, k), chip(1, k - 1)
        for part in (0, 1):
            arrived(part, near, c)
            if k == 1:
                send(part, near, z_in, when=inside)
            else:
                send(part, near, z_out, when=inside)
            send(part, near, y_dev)
            if part == 0:
                send(part, near, x_dev, landing=2)
            send(part, near, sib)
            arrived(part, other, c)
            if part == 0:
                send(part, other, x_dev, landing=2)
            send(part, other, sib)
        if k > 1:
            from_x(0, k - 1)
            from_x(1, k - 2)
        if k == 1:
            sibling_done(mine)
            multiply(mine)
        elif k == 2:
            adapters()
        else:
            for far, j in ((0, 1), (1, 0)):
                sibling_done(chip(far, j))
                multiply(chip(far, j))
    last = chip(1, 3)
    arrived(0, last, c)
    send(0, last, x_dev, landing=2)
    send(0, last, sib)
    arrived(1, last, c)
    send(1, last, sib)
    for far, j in ((0, 3), (1, 2)):
        from_x(far, j)
    for far, j in ((0, 2), (1, 1), (0, 3), (1, 2)):
        sibling_done(chip(far, j))
        multiply(chip(far, j))
    from_x(1, 3)
    sibling_done(last)
    cols = pl.ds(pl.multiple_of(last * 2 * depth, 2 * depth), 2 * depth)

    def finish(j, carry):
        at = pl.ds(pl.multiple_of(j * 256, 256), 256)
        total = acc[:, at] + jnp.dot(
            tok[:, cols], wfull[last, :, at], preferred_element_type=jnp.float32
        )
        out_ref[:, at] = total.astype(out_ref.dtype)
        return carry

    lax.fori_loop(0, width // 256, finish, 0)

    for copy, when in pending:
        if when is None:
            copy.wait_send()
        else:
            pl.when(when)(copy.wait_send)

    def sent(i, carry):
        for copy in adapter_copies(i, lax.rem(me + i, 16), me):
            copy.wait_send()
        return carry

    lax.fori_loop(1, 16, sent, 0)


def fused_body(tokens, weight, down, up, request_adapter, adapter_table_row, lengths):
    rows, model = tokens.shape
    depth, width = weight.shape
    per = lengths.shape[0]
    rank = down.shape[2]
    adapters = down.shape[0]
    requests = request_adapter.shape[0]
    part = up.shape[1]
    bf16 = jnp.bfloat16
    any_space = pl.BlockSpec(memory_space=pl.ANY)
    scalars = pl.BlockSpec(memory_space=pltpu.SMEM)
    out = pl.pallas_call(
        gather_kernel,
        out_shape=jax.ShapeDtypeStruct((rows, width), bf16),
        in_specs=[scalars, scalars] + [any_space] * 4,
        out_specs=pl.BlockSpec(memory_space=pltpu.VMEM),
        scratch_shapes=[
            pltpu.VMEM((8, 2 * depth, width), bf16),
            pltpu.VMEM((rows, model), bf16),
            pltpu.VMEM((rows, width), jnp.float32),
            pltpu.VMEM((adapters, rank, depth), bf16),
            pltpu.VMEM((adapters, rank, part), bf16),
            pltpu.VMEM((requests, rank, depth), bf16),
            pltpu.VMEM((requests, rank, part), bf16),
            pltpu.VMEM((16, per, rank, depth), bf16),
            pltpu.VMEM((16, per, rank, part), bf16),
            pltpu.VMEM((per * rank, width), bf16),
            pltpu.VMEM((rows, per * rank), jnp.float32),
            pltpu.SemaphoreType.DMA((4,)),
            pltpu.SemaphoreType.DMA((3, 8, 2)),
            pltpu.SemaphoreType.DMA((72,)),
            pltpu.SemaphoreType.DMA((2, 16)),
            pltpu.SemaphoreType.DMA((2, 16)),
        ],
        compiler_params=pltpu.CompilerParams(
            collective_id=0, has_side_effects=True, vmem_limit_bytes=52 * 2**20
        ),
        cost_estimate=pl.CostEstimate(
            flops=2 * rows * model * width, bytes_accessed=2 * rows * model, transcendentals=0
        ),
    )(
        request_adapter,
        adapter_table_row,
        tokens,
        weight,
        jnp.swapaxes(down, 1, 2),
        jnp.swapaxes(up, 1, 2),
    )
    span = rows // per
    place = jnp.arange(span, dtype=jnp.int32)
    live = (place[None, :] < lengths[:, None]).reshape(rows, 1)
    return jnp.where(live, out, jnp.zeros_like(out))


def plain_body(
    tokens,
    key_value_weight,
    adapter_down_weight,
    adapter_up_weight,
    request_adapter,
    adapter_table_row,
    lengths,
):
    per_device = lengths.shape[0]
    row_span = tokens.shape[0] // per_device
    width = tokens.shape[1]
    slot_rows = adapter_table_row[request_adapter]
    base_part = jnp.dot(
        tokens,
        lax.all_gather(key_value_weight, "req", axis=0, tiled=True),
        preferred_element_type=jnp.float32,
    )
    down_transfer = adapter_down_weight[slot_rows]
    up_transfer = adapter_up_weight[slot_rows]
    down_maps, up_maps = (
        lax.all_to_all(down_transfer, "req", split_axis=0, concat_axis=1, tiled=True),
        lax.all_to_all(up_transfer, "req", split_axis=0, concat_axis=1, tiled=True),
    )
    grouped = tokens.reshape(per_device, row_span, width)
    reduced = jnp.einsum(
        "qtd,qdk->qtk", grouped, down_maps, preferred_element_type=jnp.float32
    ).astype(jnp.bfloat16)
    adapter_term = jnp.einsum("qtk,qwk->qtw", reduced, up_maps, preferred_element_type=jnp.float32)
    adapter_term = adapter_term.reshape(tokens.shape[0], key_value_weight.shape[1])
    position = jnp.arange(row_span, dtype=jnp.int32)
    live_rows = (position[None, :] < lengths[:, None]).reshape(tokens.shape[0], 1)
    mixed = jnp.where(live_rows, base_part + 0.5 * adapter_term, jnp.zeros_like(base_part))
    return mixed.astype(jnp.bfloat16)


def solution(mesh):
    placed = (
        P(("grp", "req"), None),
        P("req", None),
        P(None, "req", None),
        P(None, "req", None),
        P("grp"),
        P(),
        P(("grp", "req")),
    )
    routed = mesh.shape["grp"] == 2 and mesh.shape["req"] == 16
    return jax.shard_map(
        fused_body if routed else plain_body,
        mesh=mesh,
        in_specs=placed,
        out_specs=P(("grp", "req"), None),
        check_vma=False,
    )
```

```python
import jax
import jax.numpy as jnp
from jax import lax
from jax.experimental import pallas as pl
from jax.experimental.pallas import tpu as pltpu
from jax.sharding import PartitionSpec as P

MESH = pl.DeviceIdType.MESH
SLOTS = 8
SIDE = 3
SHIP = 3
VM = 60
REDUCE = ((12, (0, 8)), (17, (8, 16)), (18, None))
SENDS = 32 * SLOTS


def gather_kernel(
    req_hbm, table_hbm, len_hbm, tok_hbm, w_hbm, down_hbm, up_hbm, out_ref,
    req_ref, table_ref, len_ref,
    wfull, tok, acc, down_tab, up_tab, down_stage, up_stage, down_in, up_in, up_all, red,
    local_sem, recv_sem, send_sem, ad_send, ad_recv,
):
    depth, width = w_hbm.shape
    rows = tok.shape[0]
    per = req_ref.shape[0] // 16
    rank = down_tab.shape[1]
    len_count = len_hbm.shape[0]
    tile_width = width // 4
    strip = depth // SLOTS
    side = SIDE
    mid = SLOTS - 2 * side
    x = lax.axis_index("grp")
    me = lax.axis_index("req")
    c = lax.rem(me, 2)
    y = lax.rem(lax.div(me, 2), 2)
    z = lax.div(me, 4)
    flip = lax.div(z, 2)
    zz = z + flip * (3 - 2 * z)
    inner = z + 1 - 2 * flip
    outer = z - 1 + 2 * flip
    inside = zz == 1
    order = []
    for o in (zz, 1 - zz, 2, 3):
        order.append(o + flip * (3 - 2 * o))

    def chip(far, k):
        yy = (1 - y) if far else y
        return order[k] * 2 + yy

    def device(xx, yy, zz_, cc):
        return (xx, (zz_ * 2 + yy) * 2 + cc)

    z_in = device(x, y, inner, c)
    z_out = device(x, y, outer, c)
    y_dev = device(x, 1 - y, z, c)
    x_dev = device(1 - x, y, z, c)
    sib = device(x, y, z, 1 - c)

    tok_copy = pltpu.make_async_copy(tok_hbm, tok, local_sem.at[0])
    own_rows = wfull.at[chip(0, 0), pl.ds(pl.multiple_of(c * depth, depth), depth)]
    own_copy = pltpu.make_async_copy(w_hbm, own_rows, local_sem.at[1])
    down_copy = pltpu.make_async_copy(down_hbm, down_tab, local_sem.at[2])
    up_copy = pltpu.make_async_copy(up_hbm, up_tab, local_sem.at[3])
    scalar_copies = [
        pltpu.make_async_copy(src, dst, local_sem.at[4 + i])
        for i, (src, dst) in enumerate(
            ((req_hbm, req_ref), (table_hbm, table_ref), (len_hbm, len_ref))
        )
    ]
    for copy in scalar_copies:
        copy.start()
    down_copy.start()
    up_copy.start()
    own_copy.start()
    tok_copy.start()

    barrier = pltpu.get_barrier_semaphore()

    def greet(i, carry):
        pl.semaphore_signal(
            barrier, inc=1, device_id=(x, lax.rem(me + i, 16)), device_id_type=MESH
        )
        return carry

    lax.fori_loop(1, 16, greet, 0)
    pl.semaphore_signal(barrier, inc=1, device_id=x_dev, device_id_type=MESH)
    pl.semaphore_wait(barrier, 16)

    pending = []

    def piece(slot, m, cc):
        at = pl.multiple_of(cc * depth + slot * strip, strip)
        return wfull.at[m, pl.ds(at, strip)]

    def begin(copy, when):
        pending.append((copy, when))
        if when is None:
            copy.start()
        else:
            pl.when(when)(copy.start)

    def send(slot, m, dev, own=False, when=None):
        here = piece(slot, m, c)
        src = w_hbm.at[pl.ds(pl.multiple_of(slot * strip, strip), strip)] if own else here
        copy = pltpu.make_async_remote_copy(
            src_ref=src,
            dst_ref=here,
            send_sem=send_sem.at[len(pending)],
            recv_sem=recv_sem.at[slot, m, c],
            device_id=dev,
            device_id_type=MESH,
        )
        begin(copy, when)

    def arrived(slot, m, cc):
        here = piece(slot, m, cc)
        pltpu.make_async_remote_copy(
            src_ref=here,
            dst_ref=here,
            send_sem=send_sem.at[0],
            recv_sem=recv_sem.at[slot, m, cc],
            device_id=sib,
            device_id_type=MESH,
        ).wait_recv()

    def share_own(m, cc):
        return pltpu.make_async_remote_copy(
            src_ref=w_hbm,
            dst_ref=wfull.at[m, pl.ds(pl.multiple_of(cc * depth, depth), depth)],
            send_sem=send_sem.at[len(pending)],
            recv_sem=recv_sem.at[0, m, cc],
            device_id=sib,
            device_id_type=MESH,
        )

    def sibling_done(m):
        for slot in range(SLOTS):
            arrived(slot, m, 1 - c)

    sides = [x * (side + mid) + j for j in range(side)]
    others = [(1 - x) * (side + mid) + j for j in range(side)]
    middle = [side + j for j in range(mid)]

    mine = chip(0, 0)
    for slot in sides + middle:
        send(slot, mine, z_in, own=True)
        send(slot, mine, z_out, own=True, when=inside)
        send(slot, mine, y_dev, own=True)
    begin(share_own(mine, c), None)

    for copy in scalar_copies:
        copy.wait()
    down_copy.wait()
    up_copy.wait()

    def pick(q, carry):
        row = table_ref[req_ref[q]]
        down_stage[q] = down_tab[row]
        up_stage[q] = up_tab[row]
        return carry

    lax.fori_loop(0, per * 16, pick, 0)

    def adapter_copies(i, dest, source):
        to = pl.ds(dest * per, per)
        return (
            pltpu.make_async_remote_copy(
                src_ref=down_stage.at[to],
                dst_ref=down_in.at[source],
                send_sem=ad_send.at[0, i],
                recv_sem=ad_recv.at[0, source],
                device_id=(x, dest),
                device_id_type=MESH,
            ),
            pltpu.make_async_remote_copy(
                src_ref=up_stage.at[to],
                dst_ref=up_in.at[source],
                send_sem=ad_send.at[1, i],
                recv_sem=ad_recv.at[1, source],
                device_id=(x, dest),
                device_id_type=MESH,
            ),
        )

    def ship(i, carry):
        for copy in adapter_copies(i, lax.rem(me + i, 16), me):
            copy.start()
        return carry

    down_in[me] = down_stage[pl.ds(me * per, per)]
    up_in[me] = up_stage[pl.ds(me * per, per)]
    acc[...] = jnp.zeros_like(acc)
    red[...] = jnp.zeros_like(red)
    own_copy.wait()
    tok_copy.wait()

    def ship_all():
        lax.fori_loop(1, 16, ship, 0)

    def reduce(s, carry):
        @pl.when(s != me)
        def _():
            for copy in adapter_copies(0, me, s):
                copy.wait_recv()

        cols = pl.ds(pl.multiple_of(s * depth, depth), depth)
        red[...] += lax.dot_general(
            tok[:, cols],
            down_in[s].reshape(per * rank, depth),
            (((1,), (1,)), ((), ())),
            preferred_element_type=jnp.float32,
        )
        return carry

    def reduces(first, last):
        return lambda: lax.fori_loop(first, last, reduce, 0)

    def adapters():
        span = rows // per
        row_request = lax.broadcasted_iota(jnp.int32, red.shape, 0) // span
        map_request = lax.broadcasted_iota(jnp.int32, red.shape, 1) // rank
        kept = jnp.where(row_request == map_request, red[...], 0.0).astype(jnp.bfloat16)
        part = up_in.shape[3]
        for s in range(0, 16, 2):
            pair = [up_in[s + j].reshape(per * rank, part) for j in range(2)]
            up_all[:, s * part:(s + 2) * part] = jnp.concatenate(pair, axis=1)

        def tile(j, carry):
            at = pl.ds(pl.multiple_of(j * 256, 256), 256)
            acc[:, at] += 0.5 * jnp.dot(
                kept, up_all[:, at], preferred_element_type=jnp.float32
            )
            return carry

        lax.fori_loop(0, width // 256, tile, 0)

    def tiles(m, first, last):
        cols = pl.ds(pl.multiple_of(m * 2 * depth, 2 * depth), 2 * depth)

        def tile(j, carry):
            at = pl.ds(pl.multiple_of(j * tile_width, tile_width), tile_width)
            acc[:, at] += jnp.dot(
                tok[:, cols], wfull[m, :, at], preferred_element_type=jnp.float32
            )
            return carry

        lax.fori_loop(first, last, tile, 0)

    crossing = []
    run = side + mid
    for k in range(4):
        for j in range(side):
            if k < 3:
                crossing.append((chip(0, k + 1), others[j]))
            crossing.append((chip(1, k), others[j]))

    def from_x():
        m, slot = crossing.pop(0)
        arrived(slot, m, c)
        send(slot, m, sib)

    def near_strip(k, j):
        slot, m = (sides + middle)[j], chip(0, k)
        arrived(slot, m, c)
        send(slot, m, z_in if k == 1 else z_out, when=inside)
        send(slot, m, y_dev)
        if j < side:
            send(slot, m, x_dev)
        send(slot, m, sib)

    def far_strip(k, j):
        slot, m = (sides + middle)[j], chip(1, k)
        arrived(slot, m, c)
        if j < side:
            send(slot, m, x_dev)
        send(slot, m, sib)

    half = width // tile_width // 2
    work = {
        1: lambda: (share_own(mine, 1 - c).wait_recv(), tiles(mine, 0, half)),
        2: lambda: tiles(mine, half, 2 * half),
        SHIP: ship_all,
    }
    for t, job in REDUCE:
        work[t] = adapters if job is None else reduces(*job)

    def plan(t, m):
        work[t] = lambda: (sibling_done(m), tiles(m, 0, half))
        work[t + 1] = lambda: tiles(m, half, 2 * half)

    for t, far, k in ((8, 0, 1), (10, 1, 0), (13, 0, 2), (15, 1, 1), (19, 0, 3)):
        plan(t, chip(far, k))

    for t in range(4 * run):
        if t < 3 * run:
            near_strip(t // run + 1, t % run)
        far_strip(t // run, t % run)
        if t >= 1:
            from_x()
        if t + 1 in work:
            work[t + 1]()
    while len(crossing) > side:
        from_x()
    m = chip(1, 2)
    sibling_done(m)
    tiles(m, 0, 2 * half)
    while crossing:
        from_x()
    last = chip(1, 3)
    sibling_done(last)
    cols = pl.ds(pl.multiple_of(last * 2 * depth, 2 * depth), 2 * depth)
    rows_at = lax.broadcasted_iota(jnp.int32, (rows, 1), 0)
    bound = jnp.full((rows, 1), len_ref[0], jnp.int32)
    span = rows // len_count
    for r in range(1, len_count):
        bound = jnp.where(rows_at < r * span, bound, len_ref[r] + r * span)
    live = rows_at < bound

    def finish(j, carry):
        at = pl.ds(pl.multiple_of(j * tile_width, tile_width), tile_width)
        total = acc[:, at] + jnp.dot(
            tok[:, cols], wfull[last, :, at], preferred_element_type=jnp.float32
        )
        out_ref[:, at] = jnp.where(live, total, 0.0).astype(out_ref.dtype)
        return carry

    lax.fori_loop(0, 2 * half, finish, 0)

    for copy, when in pending:
        if when is None:
            copy.wait_send()
        else:
            pl.when(when)(copy.wait_send)

    def sent(i, carry):
        for copy in adapter_copies(i, lax.rem(me + i, 16), me):
            copy.wait_send()
        return carry

    lax.fori_loop(1, 16, sent, 0)


def fused_body(tokens, weight, down, up, request_adapter, adapter_table_row, lengths):
    rows, model = tokens.shape
    depth, width = weight.shape
    per = lengths.shape[0]
    rank = down.shape[2]
    adapters = down.shape[0]
    requests = request_adapter.shape[0]
    part = up.shape[1]
    bf16 = jnp.bfloat16
    any_space = pl.BlockSpec(memory_space=pl.ANY)
    return pl.pallas_call(
        gather_kernel,
        out_shape=jax.ShapeDtypeStruct((rows, width), bf16),
        in_specs=[any_space] * 7,
        out_specs=pl.BlockSpec(memory_space=pltpu.VMEM),
        scratch_shapes=[
            pltpu.SMEM(request_adapter.shape, jnp.int32),
            pltpu.SMEM(adapter_table_row.shape, jnp.int32),
            pltpu.SMEM(lengths.shape, jnp.int32),
            pltpu.VMEM((8, 2 * depth, width), bf16),
            pltpu.VMEM((rows, model), bf16),
            pltpu.VMEM((rows, width), jnp.float32),
            pltpu.VMEM((adapters, rank, depth), bf16),
            pltpu.VMEM((adapters, rank, part), bf16),
            pltpu.VMEM((requests, rank, depth), bf16),
            pltpu.VMEM((requests, rank, part), bf16),
            pltpu.VMEM((16, per, rank, depth), bf16),
            pltpu.VMEM((16, per, rank, part), bf16),
            pltpu.VMEM((per * rank, width), bf16),
            pltpu.VMEM((rows, per * rank), jnp.float32),
            pltpu.SemaphoreType.DMA((7,)),
            pltpu.SemaphoreType.DMA((SLOTS, 8, 2)),
            pltpu.SemaphoreType.DMA((SENDS,)),
            pltpu.SemaphoreType.DMA((2, 16)),
            pltpu.SemaphoreType.DMA((2, 16)),
        ],
        compiler_params=pltpu.CompilerParams(
            collective_id=0, has_side_effects=True, vmem_limit_bytes=VM * 2**20
        ),
        cost_estimate=pl.CostEstimate(
            flops=2 * rows * model * width, bytes_accessed=2 * rows * model, transcendentals=0
        ),
    )(
        request_adapter,
        adapter_table_row,
        lengths,
        tokens,
        weight,
        jnp.swapaxes(down, 1, 2),
        jnp.swapaxes(up, 1, 2),
    )


def plain_body(
    tokens,
    key_value_weight,
    adapter_down_weight,
    adapter_up_weight,
    request_adapter,
    adapter_table_row,
    lengths,
):
    per_device = lengths.shape[0]
    row_span = tokens.shape[0] // per_device
    width = tokens.shape[1]
    slot_rows = adapter_table_row[request_adapter]
    base_part = jnp.dot(
        tokens,
        lax.all_gather(key_value_weight, "req", axis=0, tiled=True),
        preferred_element_type=jnp.float32,
    )
    down_transfer = adapter_down_weight[slot_rows]
    up_transfer = adapter_up_weight[slot_rows]
    down_maps, up_maps = (
        lax.all_to_all(down_transfer, "req", split_axis=0, concat_axis=1, tiled=True),
        lax.all_to_all(up_transfer, "req", split_axis=0, concat_axis=1, tiled=True),
    )
    grouped = tokens.reshape(per_device, row_span, width)
    reduced = jnp.einsum(
        "qtd,qdk->qtk", grouped, down_maps, preferred_element_type=jnp.float32
    ).astype(jnp.bfloat16)
    adapter_term = jnp.einsum("qtk,qwk->qtw", reduced, up_maps, preferred_element_type=jnp.float32)
    adapter_term = adapter_term.reshape(tokens.shape[0], key_value_weight.shape[1])
    position = jnp.arange(row_span, dtype=jnp.int32)
    live_rows = (position[None, :] < lengths[:, None]).reshape(tokens.shape[0], 1)
    mixed = jnp.where(live_rows, base_part + 0.5 * adapter_term, jnp.zeros_like(base_part))
    return mixed.astype(jnp.bfloat16)


def solution(mesh):
    placed = (
        P(("grp", "req"), None),
        P("req", None),
        P(None, "req", None),
        P(None, "req", None),
        P("grp"),
        P(),
        P(("grp", "req")),
    )
    routed = mesh.shape["grp"] == 2 and mesh.shape["req"] == 16
    return jax.shard_map(
        fused_body if routed else plain_body,
        mesh=mesh,
        in_specs=placed,
        out_specs=P(("grp", "req"), None),
        check_vma=False,
    )
```
